32 devices in a mesh: kpair: 4 (over x, core), band: 2 (over y), pencil: 4 (over z).
Axes of the slice: x: 2, y: 2, z: 4, core: 2. Of those that a mesh axis runs over, the one named last changes fastest.
Arguments:
- orbitals: float32 [2, 4, 2, 96, 9216], P(None, 'kpair', 'band', 'pencil'), may hold values from -6 to 6
- kcoords: int32 [4, 3], replicated, may hold values from 0 to 3, as said below
Outputs:
- exchange_vectors: float32 [2, 4, 2, 96, 9216], P(None, 'kpair', 'band', 'pencil')
The draws below stay inside these ranges and needn't reach their ends.
Inputs may be any that keep to these rules, and one draw needn't show every extreme that they name: `kcoords`: each row is a point of a 4 x 4 x 4 k-point grid given by three integer coordinates; the rows are distinct.
All inputs are finite; a program needn't handle non-finite values.
Results may differ from the reference program's by a relative error of at most 0.0001.
Values sent between devices are 32-bit elements; how exact they have to be, the bound alone decides.
A program may use at most 128 MiB of HBM per device.

```python
import math
import jax
import jax.numpy as jnp
from jax import lax

GRID = 96
NB = 2
KPTS = 4


def draw_kcoords(key, part):
    shuffled = jax.random.permutation(key, 64)
    place_high = jnp.argmax(shuffled == 63)
    shuffled = shuffled.at[place_high].set(shuffled[0]).at[0].set(63)
    place_low = jnp.argmax(shuffled == 0)
    shuffled = shuffled.at[place_low].set(shuffled[1]).at[1].set(0)
    chosen = shuffled[:KPTS]
    return jnp.stack([chosen // 16, chosen // 4 % 4, chosen % 4], axis=1).astype(jnp.int32)


def steps_of(key, shape, shards, low, largest):
    gain = 1.0
    for position, parts in shards:
        heights = jax.random.uniform(jax.random.fold_in(jax.random.fold_in(key, 6), position), (parts,), jnp.float32, low / len(shards), largest / len(shards))
        gain = gain * jnp.repeat(jnp.exp(heights), shape[position] // parts).reshape((-1,) + (1,) * (len(shape) - 1 - position))
    return gain


def normal_values(rng, shape, width, reach, shards=(), kind=jnp.bfloat16):
    values = width * jax.random.normal(rng, shape, jnp.float32)
    if shards:
        values = values * steps_of(rng, shape, shards, -0.22, 0.18)
    return jnp.clip(values, -reach, reach).astype(kind)


def setup_inputs(seed: int = 0) -> dict:
    seeds = jax.random.split(jax.random.key(seed), 3)
    return {
        "orbitals": normal_values(seeds[0], (2, KPTS, NB, GRID, GRID * GRID), 1.0, 6.0, ((1, 4), (2, 2), (3, 4)), jnp.float32),
        "kcoords": draw_kcoords(jax.random.fold_in(seeds[2], 71), 0),
    }


screening = 0.5


def frequencies():
    positions = jnp.arange(GRID)
    return jnp.where(positions < GRID // 2, positions, positions - GRID).astype(jnp.float32)


def coulomb_grid(shift_vector, along_x, along_y, along_z):
    squared = (along_x[:, None, None] + shift_vector[0]) ** 2
    squared = squared + (along_y[None, :, None] + shift_vector[1]) ** 2
    squared = squared + (along_z[None, None, :] + shift_vector[2]) ** 2
    radius = GRID // 2 - 1
    factor = (2.0 * math.pi / GRID) ** 2
    return jnp.where(squared <= radius * radius, 4.0 * math.pi / (factor * squared + screening), 0.0)


def reference(orbitals, kcoords):
    kpts = kcoords.shape[0]
    fields = lax.complex(orbitals[0], orbitals[1]).reshape(kpts, NB, GRID, GRID, GRID)
    frequency = frequencies()
    coords = kcoords.astype(jnp.float32) * 0.25
    weight = -1.0 / (kpts * NB)
    results = []
    for kpoint in range(kpts):
        own_fields = fields[kpoint]
        running = jnp.zeros_like(own_fields)
        for target in range(kpts):
            far_fields = fields[target]
            coulomb = coulomb_grid(coords[kpoint] - coords[target], frequency, frequency, frequency)
            density = jnp.conj(far_fields)[None] * own_fields[:, None]
            spectrum = jnp.fft.fftn(density, axes=(2, 3, 4))
            potential = jnp.fft.ifftn(coulomb * spectrum, axes=(2, 3, 4))
            running = running + jnp.sum(far_fields[None] * potential, axis=1)
        results.append(weight * running)
    stacked = jnp.stack(results)
    output = jnp.stack([jnp.real(stacked), jnp.imag(stacked)])
    return output.reshape(2, kpts, NB, GRID, GRID * GRID).astype(jnp.float32)
```

```python
import functools
import math

import jax
import jax.numpy as jnp
import ml_dtypes
import numpy as np
from jax import lax
from jax.experimental import pallas as pl
from jax.experimental.pallas import tpu as pltpu
from jax.sharding import PartitionSpec as P

SCREENING = 0.5
CHUNKS = 4
LANES = 128
VMEM = 48 * 1024 * 1024


def splits(table):
    high = table.astype(np.float32).astype(ml_dtypes.bfloat16)
    low = (table - high.astype(np.float64)).astype(np.float32).astype(ml_dtypes.bfloat16)
    return jnp.asarray(high), jnp.asarray(low)


def tables(grid):
    n = np.arange(grid)
    angle = (n[:, None] * n[None, :] % grid) * (2.0 * math.pi / grid)
    c, s = np.cos(angle), np.sin(angle)
    left = np.block([[c, s], [-s, c]])
    left_inverse = np.block([[c, -s], [s, c]])
    padded = -(-grid // LANES) * LANES

    def right(sine):
        table = np.zeros((2 * padded, 2 * padded))
        table[:grid, :grid] = c
        table[:grid, padded : padded + grid] = -sine
        table[padded : padded + grid, :grid] = sine
        table[padded : padded + grid, padded : padded + grid] = c
        return table

    return [splits(t) for t in (left, left_inverse, right(s), right(-s))]


def halves(x):
    high = x.astype(jnp.bfloat16)
    return high, (x - high.astype(jnp.float32)).astype(jnp.bfloat16)


def dot(a, b):
    return jnp.dot(a, b, preferred_element_type=jnp.float32)


def product(a, b):
    return dot(a[0], b[0]) + (dot(a[0], b[1]) + dot(a[1], b[0]))


def density_kernel(flag_ref, high_ref, low_ref, own_ref, far_ref, out_ref):
    rows = own_ref.shape[1]
    gr, gi = own_ref[0], own_ref[1]
    hr, hi = far_ref[0], far_ref[1]
    packed = flag_ref[0] > 0
    real = jnp.where(packed, gr * gr + gi * gi, hr * gr + hi * gi)
    imag = jnp.where(packed, hr * hr + hi * hi, hr * gi - hi * gr)
    result = product(
        (high_ref[...], low_ref[...]), halves(jnp.concatenate([real, imag], axis=0))
    )
    out_ref[0] = result[:rows]
    out_ref[1] = result[rows:]


def apply_kernel(flag_ref, high_ref, low_ref, pot_ref, own_ref, far_ref, direct_ref, reverse_ref):
    rows = own_ref.shape[1]
    pot = product(
        (high_ref[...], low_ref[...]),
        halves(jnp.concatenate([pot_ref[0], pot_ref[1]], axis=0)),
    )
    vr, vi = pot[:rows], pot[rows:]
    gr, gi = own_ref[0], own_ref[1]
    hr, hi = far_ref[0], far_ref[1]
    packed = flag_ref[0] > 0
    direct_ref[0] = jnp.where(packed, gr * vr, hr * vr - hi * vi)
    direct_ref[1] = jnp.where(packed, gi * vr, hr * vi + hi * vr)
    reverse_ref[0] = jnp.where(packed, hr * vi, gr * vr + gi * vi)
    reverse_ref[1] = jnp.where(packed, hi * vi, gi * vr - gr * vi)


def filter_kernel(grid, scale, shift_ref, *refs):
    tables_refs, refs = refs[:8], refs[8:]
    left, left_inverse, right, right_inverse = [
        (tables_refs[2 * i][...], tables_refs[2 * i + 1][...]) for i in range(4)
    ]
    count = len(refs) // 2
    ins, outs = refs[:count], refs[count:]
    planes, part, padded = ins[0].shape[1:]
    columns = [
        jnp.concatenate([r[c, i] for c in range(2) for r in ins], axis=0) for i in range(planes)
    ]
    field = product(left, halves(jnp.concatenate(columns, axis=1)))

    def to_rows(f):
        return jnp.concatenate(
            [
                jnp.concatenate(
                    [
                        f[c * grid : (c + 1) * grid, i * padded : (i + 1) * padded]
                        for c in range(2)
                    ],
                    axis=1,
                )
                for i in range(planes)
            ],
            axis=0,
        )

    field = product(halves(to_rows(field)), right)

    def frequency(index):
        return jnp.where(index < grid // 2, index, index - grid).astype(jnp.float32)

    first = pl.program_id(0) * planes
    ky = frequency(lax.broadcasted_iota(jnp.int32, (grid, padded), 0)) + shift_ref[1]
    kz = frequency(lax.broadcasted_iota(jnp.int32, (grid, padded), 1)) + shift_ref[2]
    radius = grid // 2 - 1
    factor = (2.0 * math.pi / grid) ** 2
    filters = []
    for i in range(planes):
        kx = frequency(jnp.full((grid, padded), first + i, jnp.int32)) + shift_ref[0]
        squared = kx * kx + ky * ky + kz * kz
        filters.append(
            jnp.where(
                squared <= radius * radius,
                (4.0 * math.pi * scale) / (factor * squared + SCREENING),
                0.0,
            )
        )
    coulomb = jnp.concatenate(filters, axis=0)
    field = field * jnp.concatenate([coulomb, coulomb], axis=1)
    field = product(halves(field), right_inverse)
    columns = [
        jnp.concatenate(
            [
                field[i * grid : (i + 1) * grid, c * padded : (c + 1) * padded]
                for c in range(2)
            ],
            axis=0,
        )
        for i in range(planes)
    ]
    field = product(left_inverse, halves(jnp.concatenate(columns, axis=1)))
    for c in range(2):
        for i in range(planes):
            for j, out in enumerate(outs):
                start = c * grid + j * part
                out[c, i] = field[start : start + part, i * padded : (i + 1) * padded]


def whole(array):
    return pl.BlockSpec(array.shape, lambda i: (0,) * array.ndim)


SCALARS = pl.BlockSpec(memory_space=pltpu.SMEM)


def lane_block(lanes):
    for parts in range(1, lanes + 1):
        if lanes % parts == 0 and lanes // parts % LANES == 0 and lanes // parts <= 1280:
            return lanes // parts
    return lanes


def along_x(kernel, results, flag, table, *fields):
    components, rows, lanes = fields[0].shape
    block = lane_block(lanes)
    spec = pl.BlockSpec((components, rows, block), lambda i: (0, 0, i))
    shape = jax.ShapeDtypeStruct((components, rows, lanes), jnp.float32)
    return pl.pallas_call(
        kernel,
        grid=(lanes // block,),
        in_specs=[SCALARS, whole(table[0]), whole(table[1])] + [spec] * len(fields),
        out_specs=[spec] * results,
        out_shape=[shape] * results,
        compiler_params=pltpu.CompilerParams(vmem_limit_bytes=VMEM),
        cost_estimate=pl.CostEstimate(
            flops=24 * rows * rows * lanes,
            bytes_accessed=8 * rows * lanes * (len(fields) + results),
            transcendentals=0,
        ),
    )(flag, *table, *fields)


def filtered(parts, shift, all_tables, grid, scale):
    planes = next(p for p in (8, 6, 4, 3, 2, 1) if grid % p == 0)
    flat = [t for pair in all_tables for t in pair]
    block = (2, planes) + parts[0].shape[2:]
    spec = pl.BlockSpec(block, lambda i: (0, i, 0, 0))
    return pl.pallas_call(
        functools.partial(filter_kernel, grid, scale),
        grid=(grid // planes,),
        in_specs=[SCALARS] + [whole(t) for t in flat] + [spec] * len(parts),
        out_specs=[spec] * len(parts),
        out_shape=[jax.ShapeDtypeStruct(p.shape, jnp.float32) for p in parts],
        compiler_params=pltpu.CompilerParams(vmem_limit_bytes=VMEM),
    )(shift, *flat, *parts)


def schedule(kpts, bands, sets):
    count = kpts * bands
    if count != 8 or bands != 2 or sets < 4:
        raise NotImplementedError
    x, core, y = 4, 2, 1
    rows = [
        (x, y | core, x | core, False),
        (x | core, y, core | y, False),
        (x | y, core, core | x, False),
        (x | y | core, core, core, True),
    ]
    partner = np.zeros((4, count), np.int32)
    packed = np.zeros((4, count), np.int32)
    for p, (even, odd, mask, diagonal) in enumerate(rows):
        for g in range(count):
            side = bin(g & mask).count("1") % 2
            partner[p, g] = g ^ (odd if side else even)
            packed[p, g] = int(diagonal and side == 1)
    return partner, packed


def body(orbitals, kcoords):
    kpts = kcoords.shape[0]
    bands = lax.axis_size("band") * orbitals.shape[2]
    pencils = lax.axis_size("pencil")
    slab, plane = orbitals.shape[3:]
    grid = slab * pencils
    count = kpts * bands
    partner, packed = schedule(kpts, bands, pencils)
    axes = ("kpair", "band", "pencil")
    pencil = lax.axis_index("pencil")
    orbital = lax.axis_index("kpair") * bands + lax.axis_index("band")
    row = pencil % 4
    far = jnp.asarray(partner)[row, orbital]
    flag = jnp.where(pencil < 4, jnp.asarray(packed)[row, orbital], 0).reshape(1)
    active = (pencil < 4).astype(jnp.float32)
    coords = kcoords.astype(jnp.float32) * 0.25
    shift = coords[orbital // bands] - coords[far // bands]
    shift = jnp.where(flag[0] > 0, 0.0, shift)
    fetch = [
        (int(partner[p % 4, g]) * pencils + p, g * pencils + p)
        for p in range(pencils)
        for g in range(count)
    ]
    give = [(b, a) for a, b in fetch]
    all_tables = tables(grid)
    padded = -(-grid // LANES) * LANES
    lanes = plane // CHUNKS
    part = lanes // grid

    own_chunks, far_chunks, spectra = [], [], []
    for j in range(CHUNKS):
        piece = orbitals[:, 0, 0, :, j * lanes : (j + 1) * lanes]
        own = lax.all_gather(piece, "pencil", axis=1, tiled=True)
        other = lax.ppermute(own, axes, fetch)
        own_chunks.append(own)
        far_chunks.append(other)
        (spectrum,) = along_x(density_kernel, 1, flag, all_tables[0], own, other)
        spectrum = spectrum.reshape(2, grid, part, grid)
        spectra.append(jnp.pad(spectrum, ((0, 0), (0, 0), (0, 0), (0, padded - grid))))

    scale = -1.0 / (count * grid**3)
    potentials = filtered(spectra, shift, all_tables, grid, scale)
    results = []
    for j in range(CHUNKS):
        potential = potentials[j][..., :grid].reshape(2, grid, lanes)
        direct, reverse = along_x(
            apply_kernel, 2, flag, all_tables[1], potential, own_chunks[j], far_chunks[j]
        )
        total = direct + lax.ppermute(reverse, axes, give)
        if pencils > 4:
            total = total * active
        results.append(lax.psum_scatter(total, "pencil", scatter_dimension=1, tiled=True))
    return jnp.concatenate(results, axis=2)[:, None, None]


def solution(mesh):
    in_specs = (P(None, "kpair", "band", "pencil", None), P())
    out_specs = P(None, "kpair", "band", "pencil", None)
    return jax.shard_map(body, mesh=mesh, in_specs=in_specs, out_specs=out_specs, check_vma=False)
```

```python
import functools
import math

import jax
import jax.numpy as jnp
import ml_dtypes
import numpy as np
from jax import lax
from jax.experimental import pallas as pl
from jax.experimental.pallas import tpu as pltpu
from jax.sharding import PartitionSpec as P

SCREENING = 0.5
CHUNKS = 4
LANES = 128
VMEM = 56 * 1024 * 1024
MESH = pl.DeviceIdType.MESH


def splits(table):
    high = table.astype(np.float32).astype(ml_dtypes.bfloat16)
    low = (table - high.astype(np.float64)).astype(np.float32).astype(ml_dtypes.bfloat16)
    return jnp.asarray(high), jnp.asarray(low)


def tables(grid):
    n = np.arange(grid)
    angle = (n[:, None] * n[None, :] % grid) * (2.0 * math.pi / grid)
    c, s = np.cos(angle), np.sin(angle)
    left = np.block([[c, s], [-s, c]])
    left_inverse = np.block([[c, -s], [s, c]])
    padded = -(-grid // LANES) * LANES

    def right(sine):
        table = np.zeros((2 * padded, 2 * padded))
        table[:grid, :grid] = c
        table[:grid, padded : padded + grid] = -sine
        table[padded : padded + grid, :grid] = sine
        table[padded : padded + grid, padded : padded + grid] = c
        return table

    return [splits(t) for t in (left, left_inverse, right(s), right(-s))]


def halves(x):
    high = x.astype(jnp.bfloat16)
    return high, (x - high.astype(jnp.float32)).astype(jnp.bfloat16)


def dot(a, b):
    return jnp.dot(a, b, preferred_element_type=jnp.float32)


def product(a, b):
    return dot(a[0], b[0]) + (dot(a[0], b[1]) + dot(a[1], b[0]))


def density_kernel(flag_ref, high_ref, low_ref, own_ref, far_ref, out_ref):
    rows = own_ref.shape[1]
    gr, gi = own_ref[0], own_ref[1]
    hr, hi = far_ref[0], far_ref[1]
    packed = flag_ref[0] > 0
    real = jnp.where(packed, gr * gr + gi * gi, hr * gr + hi * gi)
    imag = jnp.where(packed, hr * hr + hi * hi, hr * gi - hi * gr)
    result = product(
        (high_ref[...], low_ref[...]), halves(jnp.concatenate([real, imag], axis=0))
    )
    out_ref[0] = result[:rows]
    out_ref[1] = result[rows:]


def apply_kernel(flag_ref, high_ref, low_ref, pot_ref, own_ref, far_ref, direct_ref, reverse_ref):
    rows = own_ref.shape[1]
    pot = product(
        (high_ref[...], low_ref[...]),
        halves(jnp.concatenate([pot_ref[0], pot_ref[1]], axis=0)),
    )
    vr, vi = pot[:rows], pot[rows:]
    gr, gi = own_ref[0], own_ref[1]
    hr, hi = far_ref[0], far_ref[1]
    packed = flag_ref[0] > 0
    direct_ref[0] = jnp.where(packed, gr * vr, hr * vr - hi * vi)
    direct_ref[1] = jnp.where(packed, gi * vr, hr * vi + hi * vr)
    reverse_ref[0] = jnp.where(packed, hr * vi, gr * vr + gi * vi)
    reverse_ref[1] = jnp.where(packed, hi * vi, gi * vr - gr * vi)


def filter_kernel(grid, scale, shift_ref, *refs):
    tables_refs, refs = refs[:8], refs[8:]
    left, left_inverse, right, right_inverse = [
        (tables_refs[2 * i][...], tables_refs[2 * i + 1][...]) for i in range(4)
    ]
    ins, outs = refs
    count, _, planes, part, padded = ins.shape
    columns = [
        jnp.concatenate([ins[j, c, i] for c in range(2) for j in range(count)], axis=0)
        for i in range(planes)
    ]
    field = product(left, halves(jnp.concatenate(columns, axis=1)))

    def to_rows(f):
        return jnp.concatenate(
            [
                jnp.concatenate(
                    [
                        f[c * grid : (c + 1) * grid, i * padded : (i + 1) * padded]
                        for c in range(2)
                    ],
                    axis=1,
                )
                for i in range(planes)
            ],
            axis=0,
        )

    field = product(halves(to_rows(field)), right)

    def frequency(index):
        return jnp.where(index < grid // 2, index, index - grid).astype(jnp.float32)

    first = pl.program_id(0) * planes
    ky = frequency(lax.broadcasted_iota(jnp.int32, (grid, padded), 0)) + shift_ref[1]
    kz = frequency(lax.broadcasted_iota(jnp.int32, (grid, padded), 1)) + shift_ref[2]
    radius = grid // 2 - 1
    factor = (2.0 * math.pi / grid) ** 2
    filters = []
    for i in range(planes):
        kx = frequency(jnp.full((grid, padded), first + i, jnp.int32)) + shift_ref[0]
        squared = kx * kx + ky * ky + kz * kz
        filters.append(
            jnp.where(
                squared <= radius * radius,
                (4.0 * math.pi * scale) / (factor * squared + SCREENING),
                0.0,
            )
        )
    coulomb = jnp.concatenate(filters, axis=0)
    field = field * jnp.concatenate([coulomb, coulomb], axis=1)
    field = product(halves(field), right_inverse)
    columns = [
        jnp.concatenate(
            [
                field[i * grid : (i + 1) * grid, c * padded : (c + 1) * padded]
                for c in range(2)
            ],
            axis=0,
        )
        for i in range(planes)
    ]
    field = product(left_inverse, halves(jnp.concatenate(columns, axis=1)))
    for c in range(2):
        for i in range(planes):
            for j in range(count):
                start = c * grid + j * part
                outs[j, c, i] = field[start : start + part, i * padded : (i + 1) * padded]


def whole(array):
    return pl.BlockSpec(array.shape, lambda i: (0,) * array.ndim)


SCALARS = pl.BlockSpec(memory_space=pltpu.SMEM)


def lane_block(lanes):
    for parts in range(1, lanes + 1):
        if lanes % parts == 0 and lanes // parts % LANES == 0 and lanes // parts <= 1280:
            return lanes // parts
    return lanes


def along_x(kernel, results, flag, table, *fields):
    components, rows, lanes = fields[0].shape
    block = lane_block(lanes)
    spec = pl.BlockSpec((components, rows, block), lambda i: (0, 0, i))
    shape = jax.ShapeDtypeStruct((components, rows, lanes), jnp.float32)
    return pl.pallas_call(
        kernel,
        grid=(lanes // block,),
        in_specs=[SCALARS, whole(table[0]), whole(table[1])] + [spec] * len(fields),
        out_specs=[spec] * results,
        out_shape=[shape] * results,
        compiler_params=pltpu.CompilerParams(vmem_limit_bytes=VMEM),
        cost_estimate=pl.CostEstimate(
            flops=24 * rows * rows * lanes,
            bytes_accessed=8 * rows * lanes * (len(fields) + results),
            transcendentals=0,
        ),
    )(flag, *table, *fields)


def filtered(parts, shift, all_tables, grid, scale):
    planes = next(p for p in (8, 6, 4, 3, 2, 1) if grid % p == 0)
    flat = [t for pair in all_tables for t in pair]
    block = parts[0].shape[:2] + (planes,) + parts[0].shape[3:]
    spec = pl.BlockSpec(block, lambda i: (0, 0, i, 0, 0))
    return pl.pallas_call(
        functools.partial(filter_kernel, grid, scale),
        grid=(grid // planes,),
        in_specs=[SCALARS] + [whole(t) for t in flat] + [spec] * len(parts),
        out_specs=[spec] * len(parts),
        out_shape=[jax.ShapeDtypeStruct(p.shape, jnp.float32) for p in parts],
        compiler_params=pltpu.CompilerParams(vmem_limit_bytes=VMEM),
    )(shift, *flat, *parts)


def position():
    kpair, band, pencil = (lax.axis_index(a) for a in ("kpair", "band", "pencil"))
    x, core = kpair // 2, kpair % 2
    high, low = pencil // 2, pencil % 2
    side = (core + x * (1 - low) + band * low * (1 - high)) % 2

    def partner(side):
        flip_x = 1 - side
        flip_y = high + side * (1 - 2 * high)
        flip_core = low + side * (high + (1 - high) * (1 - low) - low)
        return {
            "kpair": (x + flip_x) % 2 * 2 + (core + flip_core) % 2,
            "band": (band + flip_y) % 2,
        }

    return pencil, partner(side), partner(1 - side)


def greet(pencil, pencils, sender, receiver):
    barrier = pltpu.get_barrier_semaphore()
    for step in (-1, 1):

        @pl.when((pencil + step >= 0) & (pencil + step < pencils))
        def _():
            pl.semaphore_signal(
                barrier, inc=1, device_id={"pencil": pencil + step}, device_id_type=MESH
            )

    pl.semaphore_signal(barrier, inc=1, device_id=sender, device_id_type=MESH)
    inner = ((pencil > 0) & (pencil < pencils - 1)).astype(jnp.int32)
    pl.semaphore_wait(barrier, 2 + inner)


def stacked(ref, chunk, component, pencils, columns):
    return jnp.concatenate([ref[chunk, q, component, :, columns] for q in range(pencils)], axis=0)


def gather_kernel(
    pencils,
    flag_ref,
    high_ref,
    low_ref,
    source,
    own_out,
    far_out,
    spectrum_out,
    own,
    far,
    spectrum,
    load_sem,
    z_send,
    z_recv,
    f_send,
    f_recv,
    own_sem,
    far_sem,
    out_sem,
):
    chunks, _, _, slab, lanes = own.shape
    grid = pencils * slab
    pencil, fetch, give = position()
    loads = [
        pltpu.make_async_copy(
            source.at[:, :, pl.ds(j * lanes, lanes)], own.at[j, pencil], load_sem.at[j]
        )
        for j in range(chunks)
    ]
    for load in loads:
        load.start()
    greet(pencil, pencils, fetch, give)

    def line(way, hop, j, q, step=None):
        step = 1 - 2 * way if step is None else step
        return pltpu.make_async_remote_copy(
            own.at[j, q],
            own.at[j, q],
            z_send.at[way, hop, j],
            z_recv.at[way, hop, j],
            device_id={"pencil": pencil + step},
            device_id_type=MESH,
        )

    def across(j, q):
        return pltpu.make_async_remote_copy(
            own.at[j, q],
            far.at[j, q],
            f_send.at[q, j],
            f_recv.at[q, j],
            device_id=give,
            device_id_type=MESH,
        )

    def sends(way, hop):
        if way == 0:
            return (pencil < pencils - 1) & (pencil >= hop)
        return (pencil > 0) & (pencil + hop < pencils)

    def receives(way, hop):
        return pencil >= hop + 1 if way == 0 else pencil + hop + 1 < pencils

    block = lane_block(lanes)

    def compute(j):
        for q in range(pencils):
            across(j, q).wait_recv()
        pltpu.make_async_copy(own.at[j], own_out.at[j], own_sem.at[j]).start()
        pltpu.make_async_copy(far.at[j], far_out.at[j], far_sem.at[j]).start()
        packed = flag_ref[0] > 0
        for b in range(lanes // block):
            columns = pl.ds(b * block, block)
            gr, gi = (stacked(own, j, c, pencils, columns) for c in range(2))
            hr, hi = (stacked(far, j, c, pencils, columns) for c in range(2))
            real = jnp.where(packed, gr * gr + gi * gi, hr * gr + hi * gi)
            imag = jnp.where(packed, hr * hr + hi * hi, hr * gi - hi * gr)
            result = product(
                (high_ref[...], low_ref[...]), halves(jnp.concatenate([real, imag], axis=0))
            )
            spectrum[j, 0, :, columns] = result[:grid]
            spectrum[j, 1, :, columns] = result[grid:]
        pltpu.make_async_copy(spectrum.at[j], spectrum_out.at[j], out_sem.at[j]).start()

    for j in range(chunks):
        loads[j].wait()
        for way in range(2):

            @pl.when(sends(way, 0))
            def _():
                line(way, 0, j, pencil).start()

        across(j, pencil).start()
    for hop in range(pencils - 1):
        for j in range(chunks):
            for way in range(2):

                @pl.when(receives(way, hop))
                def _():
                    q = pencil - (1 - 2 * way) * (hop + 1)
                    line(way, hop, j, q, 2 * way - 1).wait_recv()
                    if hop < pencils - 2:

                        @pl.when(sends(way, hop + 1))
                        def _():
                            line(way, hop + 1, j, q).start()

                    across(j, q).start()

            if hop == pencils - 2 and j > 0:
                compute(j - 1)
    compute(chunks - 1)
    for j in range(chunks):
        for hop in range(pencils - 1):
            for way in range(2):

                @pl.when(sends(way, hop))
                def _():
                    line(way, hop, j, pencil - (1 - 2 * way) * hop).wait_send()

        for q in range(pencils):
            across(j, q).wait_send()
        pltpu.make_async_copy(own.at[j], own_out.at[j], own_sem.at[j]).wait()
        pltpu.make_async_copy(far.at[j], far_out.at[j], far_sem.at[j]).wait()
        pltpu.make_async_copy(spectrum.at[j], spectrum_out.at[j], out_sem.at[j]).wait()


def scatter_kernel(
    pencils,
    flag_ref,
    high_ref,
    low_ref,
    pot_in,
    own_in,
    far_in,
    out,
    pot,
    own,
    far,
    back,
    arrived,
    load_sem,
    r_send,
    r_recv,
    z_send,
    z_recv,
    out_sem,
):
    chunks, _, _, slab, lanes = own.shape
    grid = pencils * slab
    pencil, fetch, give = position()

    def loads(j):
        return [
            pltpu.make_async_copy(a.at[j], b.at[j], load_sem.at[i, j])
            for i, (a, b) in enumerate(((pot_in, pot), (own_in, own), (far_in, far)))
        ]

    for j in range(chunks):
        for load in loads(j):
            load.start()
    greet(pencil, pencils, give, fetch)

    def across(j):
        return pltpu.make_async_remote_copy(
            far.at[j],
            back.at[j],
            r_send.at[j],
            r_recv.at[j],
            device_id=fetch,
            device_id_type=MESH,
        )

    def line(way, left, j):
        step = 1 - 2 * way
        return pltpu.make_async_remote_copy(
            own.at[j, pencil + step * (left + 1)],
            arrived.at[j, way, left],
            z_send.at[way, left, j],
            z_recv.at[way, left, j],
            device_id={"pencil": pencil + step},
            device_id_type=MESH,
        )

    def landing(way, left, j):
        return pltpu.make_async_remote_copy(
            own.at[j, pencil],
            arrived.at[j, way, left],
            z_send.at[way, left, j],
            z_recv.at[way, left, j],
            device_id={"pencil": pencil - 1 + 2 * way},
            device_id_type=MESH,
        )

    def sends(way, left):
        return pencil + left + 1 < pencils if way == 0 else pencil - left - 1 >= 0

    def has_previous(way):
        return pencil > 0 if way == 0 else pencil < pencils - 1

    block = lane_block(lanes)

    def compute(j):
        for load in loads(j):
            load.wait()
        packed = flag_ref[0] > 0
        for b in range(lanes // block):
            columns = pl.ds(b * block, block)
            field = product(
                (high_ref[...], low_ref[...]),
                halves(jnp.concatenate([pot[j, 0, :, columns], pot[j, 1, :, columns]], axis=0)),
            )
            for q in range(pencils):
                vr = field[q * slab : (q + 1) * slab]
                vi = field[grid + q * slab : grid + (q + 1) * slab]
                gr, gi = own[j, q, 0, :, columns], own[j, q, 1, :, columns]
                hr, hi = far[j, q, 0, :, columns], far[j, q, 1, :, columns]
                own[j, q, 0, :, columns] = jnp.where(packed, gr * vr, hr * vr - hi * vi)
                own[j, q, 1, :, columns] = jnp.where(packed, gi * vr, hr * vi + hi * vr)
                far[j, q, 0, :, columns] = jnp.where(packed, hr * vi, gr * vr + gi * vi)
                far[j, q, 1, :, columns] = jnp.where(packed, hi * vi, gi * vr - gr * vi)
        across(j).start()

    def finish(j):
        for way in range(2):

            @pl.when(has_previous(way))
            def _():
                landing(way, 0, j).wait_recv()
                own[j, pencil] = own[j, pencil] + arrived[j, way, 0]

        pltpu.make_async_copy(
            own.at[j, pencil], out.at[:, :, pl.ds(j * lanes, lanes)], out_sem.at[j]
        ).start()

    for j in range(chunks):
        compute(j)
    for j in range(chunks):
        across(j).wait_recv()
        for q in range(pencils):
            own[j, q] = own[j, q] + back[j, q]
        for left in range(pencils - 2, -1, -1):
            for way in range(2):

                @pl.when(sends(way, left))
                def _():
                    if left + 1 < pencils - 1:

                        @pl.when(has_previous(way))
                        def _():
                            landing(way, left + 1, j).wait_recv()
                            q = pencil + (1 - 2 * way) * (left + 1)
                            own[j, q] = own[j, q] + arrived[j, way, left + 1]

                    line(way, left, j).start()

        if j > 0:
            finish(j - 1)
    finish(chunks - 1)
    for j in range(chunks):
        across(j).wait_send()
        for left in range(pencils - 1):
            for way in range(2):

                @pl.when(sends(way, left))
                def _():
                    line(way, left, j).wait_send()

        pltpu.make_async_copy(
            own.at[j, pencil], out.at[:, :, pl.ds(j * lanes, lanes)], out_sem.at[j]
        ).wait()


ANY = pl.BlockSpec(memory_space=pl.ANY)
WHOLE = pl.BlockSpec(memory_space=pltpu.VMEM)


def gathered(piece, flag, table, pencils):
    _, slab, plane = piece.shape
    grid, lanes = slab * pencils, plane // CHUNKS
    fields = (CHUNKS, pencils, 2, slab, lanes)
    spectrum = (CHUNKS, 2, grid, lanes)
    dma = pltpu.SemaphoreType.DMA
    return pl.pallas_call(
        functools.partial(gather_kernel, pencils),
        in_specs=[SCALARS, WHOLE, WHOLE, ANY],
        out_specs=[ANY] * 3,
        out_shape=[jax.ShapeDtypeStruct(s, jnp.float32) for s in (fields, fields, spectrum)],
        scratch_shapes=[pltpu.VMEM(s, jnp.float32) for s in (fields, fields, spectrum)]
        + [
            dma((CHUNKS,)),
            dma((2, pencils - 1, CHUNKS)),
            dma((2, pencils - 1, CHUNKS)),
            dma((pencils, CHUNKS)),
            dma((pencils, CHUNKS)),
            dma((CHUNKS,)),
            dma((CHUNKS,)),
            dma((CHUNKS,)),
        ],
        compiler_params=pltpu.CompilerParams(
            collective_id=0, has_side_effects=True, vmem_limit_bytes=VMEM
        ),
    )(flag, *table, piece)


def scattered(potential, own, far, flag, table, pencils):
    _, _, _, slab, lanes = own.shape
    dma = pltpu.SemaphoreType.DMA
    arrived = (CHUNKS, 2, pencils - 1, 2, slab, lanes)
    shapes = (potential.shape, own.shape, own.shape, own.shape, arrived)
    return pl.pallas_call(
        functools.partial(scatter_kernel, pencils),
        in_specs=[SCALARS, WHOLE, WHOLE] + [ANY] * 3,
        out_specs=ANY,
        out_shape=jax.ShapeDtypeStruct((2, slab, lanes * CHUNKS), jnp.float32),
        scratch_shapes=[pltpu.VMEM(s, jnp.float32) for s in shapes]
        + [
            dma((3, CHUNKS)),
            dma((CHUNKS,)),
            dma((CHUNKS,)),
            dma((2, pencils - 1, CHUNKS)),
            dma((2, pencils - 1, CHUNKS)),
            dma((CHUNKS,)),
        ],
        compiler_params=pltpu.CompilerParams(
            collective_id=1, has_side_effects=True, vmem_limit_bytes=VMEM
        ),
    )(flag, *table, potential, own, far)


def schedule(kpts, bands, sets):
    count = kpts * bands
    if count != 8 or bands != 2 or sets < 4:
        raise NotImplementedError
    x, core, y = 4, 2, 1
    rows = [
        (x, y | core, x | core, False),
        (x | core, y, core | y, False),
        (x | y, core, core | x, False),
        (x | y | core, core, core, True),
    ]
    partner = np.zeros((4, count), np.int32)
    packed = np.zeros((4, count), np.int32)
    for p, (even, odd, mask, diagonal) in enumerate(rows):
        for g in range(count):
            side = bin(g & mask).count("1") % 2
            partner[p, g] = g ^ (odd if side else even)
            packed[p, g] = int(diagonal and side == 1)
    return partner, packed


def body(orbitals, kcoords):
    kpts = kcoords.shape[0]
    bands = lax.axis_size("band") * orbitals.shape[2]
    pencils = lax.axis_size("pencil")
    slab, plane = orbitals.shape[3:]
    grid = slab * pencils
    count = kpts * bands
    partner, packed = schedule(kpts, bands, pencils)
    axes = ("kpair", "band", "pencil")
    pencil = lax.axis_index("pencil")
    orbital = lax.axis_index("kpair") * bands + lax.axis_index("band")
    row = pencil % 4
    far = jnp.asarray(partner)[row, orbital]
    flag = jnp.where(pencil < 4, jnp.asarray(packed)[row, orbital], 0).reshape(1)
    active = (pencil < 4).astype(jnp.float32)
    coords = kcoords.astype(jnp.float32) * 0.25
    shift = coords[orbital // bands] - coords[far // bands]
    shift = jnp.where(flag[0] > 0, 0.0, shift)
    fetch = [
        (int(partner[p % 4, g]) * pencils + p, g * pencils + p)
        for p in range(pencils)
        for g in range(count)
    ]
    give = [(b, a) for a, b in fetch]
    all_tables = tables(grid)
    padded = -(-grid // LANES) * LANES
    lanes = plane // CHUNKS
    part = lanes // grid

    scale = -1.0 / (count * grid**3)

    if pencils == 4 and slab % 8 == 0:
        own, other, spectrum = gathered(orbitals[:, 0, 0], flag, all_tables[0], pencils)
        spectrum = spectrum.reshape(CHUNKS, 2, grid, part, grid)
        spectrum = jnp.pad(spectrum, ((0, 0),) * 4 + ((0, padded - grid),))
        potential = filtered([spectrum], shift, all_tables, grid, scale)[0]
        potential = potential[..., :grid].reshape(CHUNKS, 2, grid, lanes)
        result = scattered(potential, own, other, flag, all_tables[1], pencils)
        return result[:, None, None]

    own_chunks, far_chunks, spectra = [], [], []
    for j in range(CHUNKS):
        piece = orbitals[:, 0, 0, :, j * lanes : (j + 1) * lanes]
        own = lax.all_gather(piece, "pencil", axis=1, tiled=True)
        other = lax.ppermute(own, axes, fetch)
        own_chunks.append(own)
        far_chunks.append(other)
        (spectrum,) = along_x(density_kernel, 1, flag, all_tables[0], own, other)
        spectrum = spectrum.reshape(2, grid, part, grid)
        spectra.append(jnp.pad(spectrum, ((0, 0), (0, 0), (0, 0), (0, padded - grid))))

    potentials = filtered([jnp.stack(spectra)], shift, all_tables, grid, scale)[0]
    results = []
    for j in range(CHUNKS):
        potential = potentials[j][..., :grid].reshape(2, grid, lanes)
        direct, reverse = along_x(
            apply_kernel, 2, flag, all_tables[1], potential, own_chunks[j], far_chunks[j]
        )
        total = direct + lax.ppermute(reverse, axes, give)
        if pencils > 4:
            total = total * active
        results.append(lax.psum_scatter(total, "pencil", scatter_dimension=1, tiled=True))
    return jnp.concatenate(results, axis=2)[:, None, None]


def solution(mesh):
    in_specs = (P(None, "kpair", "band", "pencil", None), P())
    out_specs = P(None, "kpair", "band", "pencil", None)
    return jax.shard_map(body, mesh=mesh, in_specs=in_specs, out_specs=out_specs, check_vma=False)
```

```python
import functools
import math

import jax
import jax.numpy as jnp
import ml_dtypes
import numpy as np
from jax import lax
from jax.experimental import pallas as pl
from jax.experimental.pallas import tpu as pltpu
from jax.sharding import PartitionSpec as P

SCREENING = 0.5
CHUNKS = 6
LANES = 128
VMEM = 56 * 1024 * 1024
MESH = pl.DeviceIdType.MESH


def splits(table):
    high = table.astype(np.float32).astype(ml_dtypes.bfloat16)
    low = (table - high.astype(np.float64)).astype(np.float32).astype(ml_dtypes.bfloat16)
    return jnp.asarray(high), jnp.asarray(low)


def tables(grid):
    n = np.arange(grid)
    angle = (n[:, None] * n[None, :] % grid) * (2.0 * math.pi / grid)
    c, s = np.cos(angle), np.sin(angle)
    left = np.block([[c, s], [-s, c]])
    left_inverse = np.block([[c, -s], [s, c]])
    padded = -(-grid // LANES) * LANES

    def right(sine):
        table = np.zeros((2 * padded, 2 * padded))
        table[:grid, :grid] = c
        table[:grid, padded : padded + grid] = -sine
        table[padded : padded + grid, :grid] = sine
        table[padded : padded + grid, padded : padded + grid] = c
        return table

    return [splits(t) for t in (left, left_inverse, right(s), right(-s))]


def halves(x):
    high = x.astype(jnp.bfloat16)
    return high, (x - high.astype(jnp.float32)).astype(jnp.bfloat16)


def dot(a, b):
    return jnp.dot(a, b, preferred_element_type=jnp.float32)


def product(a, b):
    return dot(a[0], b[0]) + (dot(a[0], b[1]) + dot(a[1], b[0]))


def density_kernel(flag_ref, high_ref, low_ref, own_ref, far_ref, out_ref):
    rows = own_ref.shape[1]
    gr, gi = own_ref[0], own_ref[1]
    hr, hi = far_ref[0], far_ref[1]
    packed = flag_ref[0] > 0
    real = jnp.where(packed, gr * gr + gi * gi, hr * gr + hi * gi)
    imag = jnp.where(packed, hr * hr + hi * hi, hr * gi - hi * gr)
    result = product(
        (high_ref[...], low_ref[...]), halves(jnp.concatenate([real, imag], axis=0))
    )
    out_ref[0] = result[:rows]
    out_ref[1] = result[rows:]


def apply_kernel(flag_ref, high_ref, low_ref, pot_ref, own_ref, far_ref, direct_ref, reverse_ref):
    rows = own_ref.shape[1]
    pot = product(
        (high_ref[...], low_ref[...]),
        halves(jnp.concatenate([pot_ref[0], pot_ref[1]], axis=0)),
    )
    vr, vi = pot[:rows], pot[rows:]
    gr, gi = own_ref[0], own_ref[1]
    hr, hi = far_ref[0], far_ref[1]
    packed = flag_ref[0] > 0
    direct_ref[0] = jnp.where(packed, gr * vr, hr * vr - hi * vi)
    direct_ref[1] = jnp.where(packed, gi * vr, hr * vi + hi * vr)
    reverse_ref[0] = jnp.where(packed, hr * vi, gr * vr + gi * vi)
    reverse_ref[1] = jnp.where(packed, hi * vi, gi * vr - gr * vi)


def offset_of(coords_ref):
    _, fetch, _, diagonal = position()
    own, far = lax.axis_index("kpair"), fetch["kpair"]
    return [
        (coords_ref[own, a] - coords_ref[far, a]).astype(jnp.float32)
        * (0.25 * (1 - diagonal).astype(jnp.float32))
        for a in range(3)
    ]


def filter_kernel(grid, scale, shift_ref, *refs):
    tables_refs, refs = refs[:8], refs[8:]
    left, left_inverse, right, right_inverse = [
        (tables_refs[2 * i][...], tables_refs[2 * i + 1][...]) for i in range(4)
    ]
    ins, outs = refs
    count, _, planes, part, padded = ins.shape
    columns = [
        jnp.concatenate([ins[j, c, i] for c in range(2) for j in range(count)], axis=0)
        for i in range(planes)
    ]
    field = product(left, halves(jnp.concatenate(columns, axis=1)))

    def to_rows(f):
        return jnp.concatenate(
            [
                jnp.concatenate(
                    [
                        f[c * grid : (c + 1) * grid, i * padded : (i + 1) * padded]
                        for c in range(2)
                    ],
                    axis=1,
                )
                for i in range(planes)
            ],
            axis=0,
        )

    field = product(halves(to_rows(field)), right)

    def frequency(index):
        return jnp.where(index < grid // 2, index, index - grid).astype(jnp.float32)

    shift = [shift_ref[a] for a in range(3)] if len(shift_ref.shape) == 1 else offset_of(shift_ref)
    first = pl.program_id(0) * planes
    ky = frequency(lax.broadcasted_iota(jnp.int32, (grid, padded), 0)) + shift[1]
    kz = frequency(lax.broadcasted_iota(jnp.int32, (grid, padded), 1)) + shift[2]
    radius = grid // 2 - 1
    factor = (2.0 * math.pi / grid) ** 2
    filters = []
    for i in range(planes):
        kx = frequency(jnp.full((grid, padded), first + i, jnp.int32)) + shift[0]
        squared = kx * kx + ky * ky + kz * kz
        filters.append(
            jnp.where(
                squared <= radius * radius,
                (4.0 * math.pi * scale) / (factor * squared + SCREENING),
                0.0,
            )
        )
    coulomb = jnp.concatenate(filters, axis=0)
    field = field * jnp.concatenate([coulomb, coulomb], axis=1)
    field = product(halves(field), right_inverse)
    columns = [
        jnp.concatenate(
            [
                field[i * grid : (i + 1) * grid, c * padded : (c + 1) * padded]
                for c in range(2)
            ],
            axis=0,
        )
        for i in range(planes)
    ]
    field = product(left_inverse, halves(jnp.concatenate(columns, axis=1)))
    for c in range(2):
        for i in range(planes):
            for j in range(count):
                start = c * grid + j * part
                outs[j, c, i] = field[start : start + part, i * padded : (i + 1) * padded]


def whole(array):
    return pl.BlockSpec(array.shape, lambda i: (0,) * array.ndim)


SCALARS = pl.BlockSpec(memory_space=pltpu.SMEM)


def lane_block(lanes):
    for parts in range(1, lanes + 1):
        if lanes % parts == 0 and lanes // parts % LANES == 0 and lanes // parts <= 1280:
            return lanes // parts
    return lanes


def row_block(lanes, grid):
    step = math.lcm(grid, LANES)
    fits = [b for b in range(step, 1281, step) if lanes % b == 0]
    return fits[-1] if fits else lanes


def along_x(kernel, results, flag, table, *fields):
    components, rows, lanes = fields[0].shape
    block = lane_block(lanes)
    spec = pl.BlockSpec((components, rows, block), lambda i: (0, 0, i))
    shape = jax.ShapeDtypeStruct((components, rows, lanes), jnp.float32)
    return pl.pallas_call(
        kernel,
        grid=(lanes // block,),
        in_specs=[SCALARS, whole(table[0]), whole(table[1])] + [spec] * len(fields),
        out_specs=[spec] * results,
        out_shape=[shape] * results,
        compiler_params=pltpu.CompilerParams(vmem_limit_bytes=VMEM),
        cost_estimate=pl.CostEstimate(
            flops=24 * rows * rows * lanes,
            bytes_accessed=8 * rows * lanes * (len(fields) + results),
            transcendentals=0,
        ),
    )(flag, *table, *fields)


def filtered(parts, shift, all_tables, grid, scale):
    planes = next(p for p in (8, 6, 4, 3, 2, 1) if grid % p == 0)
    flat = [t for pair in all_tables for t in pair]
    block = parts[0].shape[:2] + (planes,) + parts[0].shape[3:]
    spec = pl.BlockSpec(block, lambda i: (0, 0, i, 0, 0))
    return pl.pallas_call(
        functools.partial(filter_kernel, grid, scale),
        grid=(grid // planes,),
        in_specs=[SCALARS] + [whole(t) for t in flat] + [spec] * len(parts),
        out_specs=[spec] * len(parts),
        out_shape=[jax.ShapeDtypeStruct(p.shape, jnp.float32) for p in parts],
        compiler_params=pltpu.CompilerParams(vmem_limit_bytes=VMEM),
    )(shift, *flat, *parts)


def position():
    kpair, band, pencil = (lax.axis_index(a) for a in ("kpair", "band", "pencil"))
    x, core = kpair // 2, kpair % 2
    high, low = pencil // 2, pencil % 2
    side = (core + x * (1 - low) + band * low * (1 - high)) % 2

    def partner(side):
        flip_x = 1 - side
        flip_y = high + side * (1 - 2 * high)
        flip_core = low + side * (high + (1 - high) * (1 - low) - low)
        return {
            "kpair": (x + flip_x) % 2 * 2 + (core + flip_core) % 2,
            "band": (band + flip_y) % 2,
        }

    return pencil, partner(side), partner(1 - side), side * high * low


def greet(pencil, pencils, sender, receiver):
    barrier = pltpu.get_barrier_semaphore()
    for step in (-1, 1):

        @pl.when((pencil + step >= 0) & (pencil + step < pencils))
        def _():
            pl.semaphore_signal(
                barrier, inc=1, device_id={"pencil": pencil + step}, device_id_type=MESH
            )

    pl.semaphore_signal(barrier, inc=1, device_id=sender, device_id_type=MESH)
    inner = ((pencil > 0) & (pencil < pencils - 1)).astype(jnp.int32)
    pl.semaphore_wait(barrier, 2 + inner)


def tile_roll(tile, amount):
    return pltpu.roll(tile, amount % LANES, 1)


def unflatten(flat, grid):
    rows = flat.shape[1] // grid
    tiles = [flat[:, t : t + LANES] for t in range(0, flat.shape[1], LANES)]
    lane = lax.broadcasted_iota(jnp.int32, tiles[0].shape, 1)
    result = []
    for y in range(rows):
        tile, offset = divmod(y * grid, LANES)
        value = tile_roll(tiles[tile], -offset) if offset else tiles[tile]
        if offset + grid > LANES:
            after = tile_roll(tiles[tile + 1], -offset)
            value = jnp.where(lane < LANES - offset, value, after)
        result.append(value)
    return result


def flatten(rows, grid):
    total = len(rows) * grid
    lane = lax.broadcasted_iota(jnp.int32, rows[0].shape, 1)
    rolled = [tile_roll(r, y * grid) if y * grid % LANES else r for y, r in enumerate(rows)]
    tiles = []
    for start in range(0, total, LANES):
        first, last = start // grid, (start + LANES - 1) // grid
        value = rolled[first]
        for y in range(first + 1, last + 1):
            value = jnp.where(lane < y * grid - start, value, rolled[y])
        tiles.append(value)
    return jnp.concatenate(tiles, axis=1)


def stacked(ref, chunk, component, pencils, columns):
    return jnp.concatenate([ref[chunk, q, component, :, columns] for q in range(pencils)], axis=0)


def gather_kernel(
    pencils,
    high_ref,
    low_ref,
    source,
    own_out,
    far_out,
    spectrum_out,
    own,
    far,
    spectrum,
    load_sem,
    z_send,
    z_recv,
    f_send,
    f_recv,
    own_sem,
    far_sem,
    out_sem,
):
    chunks, _, _, slab, lanes = own.shape
    grid = pencils * slab
    pencil, fetch, give, diagonal = position()
    loads = [
        pltpu.make_async_copy(
            source.at[:, :, pl.ds(j * lanes, lanes)], own.at[j, pencil], load_sem.at[j]
        )
        for j in range(chunks)
    ]
    for load in loads:
        load.start()
    greet(pencil, pencils, fetch, give)

    def line(way, hop, j, q, step=None):
        step = 1 - 2 * way if step is None else step
        return pltpu.make_async_remote_copy(
            own.at[j, q],
            own.at[j, q],
            z_send.at[way, hop, j],
            z_recv.at[way, hop, j],
            device_id={"pencil": pencil + step},
            device_id_type=MESH,
        )

    def across(j, q):
        return pltpu.make_async_remote_copy(
            own.at[j, q],
            far.at[j, q],
            f_send.at[q, j],
            f_recv.at[q, j],
            device_id=give,
            device_id_type=MESH,
        )

    def sends(way, hop):
        if way == 0:
            return (pencil < pencils - 1) & (pencil >= hop)
        return (pencil > 0) & (pencil + hop < pencils)

    def receives(way, hop):
        return pencil >= hop + 1 if way == 0 else pencil + hop + 1 < pencils

    block = row_block(lanes, grid)
    part = lanes // grid

    def publish(j):
        rows = pl.ds(j * part, part)
        return pltpu.make_async_copy(
            spectrum.at[:, :, rows, :], spectrum_out.at[:, :, rows, :], out_sem.at[j]
        )

    def compute(j):
        for q in range(pencils):
            across(j, q).wait_recv()
        pltpu.make_async_copy(own.at[j], own_out.at[j], own_sem.at[j]).start()
        pltpu.make_async_copy(far.at[j], far_out.at[j], far_sem.at[j]).start()
        packed = diagonal > 0
        for b in range(lanes // block):
            columns = pl.ds(b * block, block)
            gr, gi = (stacked(own, j, c, pencils, columns) for c in range(2))
            hr, hi = (stacked(far, j, c, pencils, columns) for c in range(2))
            real = jnp.where(packed, gr * gr + gi * gi, hr * gr + hi * gi)
            imag = jnp.where(packed, hr * hr + hi * hi, hr * gi - hi * gr)
            result = product(
                (high_ref[...], low_ref[...]), halves(jnp.concatenate([real, imag], axis=0))
            )
            for m, value in enumerate(unflatten(result, grid)):
                y = (j * lanes + b * block) // grid + m
                spectrum[0, :, y, :] = value[:grid]
                spectrum[1, :, y, :] = value[grid:]
        publish(j).start()

    for j in range(chunks):
        loads[j].wait()
        for way in range(2):

            @pl.when(sends(way, 0))
            def _():
                line(way, 0, j, pencil).start()

        across(j, pencil).start()
    for hop in range(pencils - 1):
        for j in range(chunks):
            for way in range(2):

                @pl.when(receives(way, hop))
                def _():
                    q = pencil - (1 - 2 * way) * (hop + 1)
                    line(way, hop, j, q, 2 * way - 1).wait_recv()
                    if hop < pencils - 2:

                        @pl.when(sends(way, hop + 1))
                        def _():
                            line(way, hop + 1, j, q).start()

                    across(j, q).start()

            if hop == pencils - 2 and j > 0:
                compute(j - 1)
    compute(chunks - 1)
    for j in range(chunks):
        for hop in range(pencils - 1):
            for way in range(2):

                @pl.when(sends(way, hop))
                def _():
                    line(way, hop, j, pencil - (1 - 2 * way) * hop).wait_send()

        for q in range(pencils):
            across(j, q).wait_send()
        pltpu.make_async_copy(own.at[j], own_out.at[j], own_sem.at[j]).wait()
        pltpu.make_async_copy(far.at[j], far_out.at[j], far_sem.at[j]).wait()
        publish(j).wait()


def scatter_kernel(
    pencils,
    high_ref,
    low_ref,
    pot_in,
    own_in,
    far_in,
    out,
    pot,
    own,
    far,
    back,
    arrived,
    load_sem,
    r_send,
    r_recv,
    z_send,
    z_recv,
    out_sem,
):
    chunks, _, _, slab, lanes = own.shape
    grid = pencils * slab
    pencil, fetch, give, diagonal = position()

    part = lanes // grid

    def loads(j):
        rows = pl.ds(j * part, part)
        pairs = [(pot_in.at[:, :, rows, :], pot.at[:, :, rows, :])]
        pairs += [(a.at[j], b.at[j]) for a, b in ((own_in, own), (far_in, far))]
        return [
            pltpu.make_async_copy(a, b, load_sem.at[i, j]) for i, (a, b) in enumerate(pairs)
        ]

    for j in range(chunks):
        for load in loads(j):
            load.start()
    greet(pencil, pencils, give, fetch)

    upper = pencil // (pencils // 2)

    def across(j, i):
        return back_of(j, upper * i + (1 - upper) * (pencils - 1 - i))

    def back_of(j, q):
        return pltpu.make_async_remote_copy(
            far.at[j, q],
            back.at[j, q],
            r_send.at[q, j],
            r_recv.at[q, j],
            device_id=fetch,
            device_id_type=MESH,
        )

    def line(way, left, j):
        step = 1 - 2 * way
        return pltpu.make_async_remote_copy(
            own.at[j, pencil + step * (left + 1)],
            arrived.at[j, way, left],
            z_send.at[way, left, j],
            z_recv.at[way, left, j],
            device_id={"pencil": pencil + step},
            device_id_type=MESH,
        )

    def landing(way, left, j):
        return pltpu.make_async_remote_copy(
            own.at[j, pencil],
            arrived.at[j, way, left],
            z_send.at[way, left, j],
            z_recv.at[way, left, j],
            device_id={"pencil": pencil - 1 + 2 * way},
            device_id_type=MESH,
        )

    def sends(way, left):
        return pencil + left + 1 < pencils if way == 0 else pencil - left - 1 >= 0

    def has_previous(way):
        return pencil > 0 if way == 0 else pencil < pencils - 1

    block = row_block(lanes, grid)

    def compute(j):
        for load in loads(j):
            load.wait()
        packed = diagonal > 0
        for b in range(lanes // block):
            columns = pl.ds(b * block, block)
            first = (j * lanes + b * block) // grid
            rows = [
                jnp.concatenate([pot[0, :, y, :], pot[1, :, y, :]], axis=0)
                for y in range(first, first + block // grid)
            ]
            field = product(
                (high_ref[...], low_ref[...]),
                halves(flatten(rows, grid)),
            )
            for q in range(pencils):
                vr = field[q * slab : (q + 1) * slab]
                vi = field[grid + q * slab : grid + (q + 1) * slab]
                gr, gi = own[j, q, 0, :, columns], own[j, q, 1, :, columns]
                hr, hi = far[j, q, 0, :, columns], far[j, q, 1, :, columns]
                own[j, q, 0, :, columns] = jnp.where(packed, gr * vr, hr * vr - hi * vi)
                own[j, q, 1, :, columns] = jnp.where(packed, gi * vr, hr * vi + hi * vr)
                far[j, q, 0, :, columns] = jnp.where(packed, hr * vi, gr * vr + gi * vi)
                far[j, q, 1, :, columns] = jnp.where(packed, hi * vi, gi * vr - gr * vi)
        for i in range(pencils):
            across(j, i).start()

    def merge(j, left, way):
        q = pencil + (1 - 2 * way) * (left + 1)
        back_of(j, q).wait_recv()
        own[j, q] = own[j, q] + back[j, q]

    def merge_own(j):
        back_of(j, pencil).wait_recv()
        own[j, pencil] = own[j, pencil] + back[j, pencil]

    def finish(j):
        merge_own(j)
        for way in range(2):

            @pl.when(has_previous(way))
            def _():
                landing(way, 0, j).wait_recv()
                own[j, pencil] = own[j, pencil] + arrived[j, way, 0]

        pltpu.make_async_copy(
            own.at[j, pencil], out.at[:, :, pl.ds(j * lanes, lanes)], out_sem.at[j]
        ).start()

    compute(0)
    for j in range(chunks):
        if j + 1 < chunks:
            compute(j + 1)
        for left in range(pencils - 2, -1, -1):
            for way in range(2):

                @pl.when(sends(way, left))
                def _():
                    merge(j, left, way)
                    if left + 1 < pencils - 1:

                        @pl.when(has_previous(way))
                        def _():
                            landing(way, left + 1, j).wait_recv()
                            q = pencil + (1 - 2 * way) * (left + 1)
                            own[j, q] = own[j, q] + arrived[j, way, left + 1]

                    line(way, left, j).start()

        if j > 0:
            finish(j - 1)
    finish(chunks - 1)
    for j in range(chunks):
        for i in range(pencils):
            across(j, i).wait_send()
        for left in range(pencils - 1):
            for way in range(2):

                @pl.when(sends(way, left))
                def _():
                    line(way, left, j).wait_send()

        pltpu.make_async_copy(
            own.at[j, pencil], out.at[:, :, pl.ds(j * lanes, lanes)], out_sem.at[j]
        ).wait()


ANY = pl.BlockSpec(memory_space=pl.ANY)
WHOLE = pl.BlockSpec(memory_space=pltpu.VMEM)


def gathered(piece, table, pencils):
    _, slab, plane = piece.shape
    grid, lanes = slab * pencils, plane // CHUNKS
    fields = (CHUNKS, pencils, 2, slab, lanes)
    spectrum = (2, grid, plane // grid, -(-grid // LANES) * LANES)
    dma = pltpu.SemaphoreType.DMA
    return pl.pallas_call(
        functools.partial(gather_kernel, pencils),
        in_specs=[WHOLE, WHOLE, ANY],
        out_specs=[ANY] * 3,
        out_shape=[jax.ShapeDtypeStruct(s, jnp.float32) for s in (fields, fields, spectrum)],
        scratch_shapes=[pltpu.VMEM(s, jnp.float32) for s in (fields, fields, spectrum)]
        + [
            dma((CHUNKS,)),
            dma((2, pencils - 1, CHUNKS)),
            dma((2, pencils - 1, CHUNKS)),
            dma((pencils, CHUNKS)),
            dma((pencils, CHUNKS)),
            dma((CHUNKS,)),
            dma((CHUNKS,)),
            dma((CHUNKS,)),
        ],
        compiler_params=pltpu.CompilerParams(
            collective_id=0, has_side_effects=True, vmem_limit_bytes=VMEM
        ),
    )(*table, piece)


def scattered(potential, own, far, table, pencils):
    _, _, _, slab, lanes = own.shape
    dma = pltpu.SemaphoreType.DMA
    arrived = (CHUNKS, 2, pencils - 1, 2, slab, lanes)
    shapes = (potential.shape, own.shape, own.shape, own.shape, arrived)
    return pl.pallas_call(
        functools.partial(scatter_kernel, pencils),
        in_specs=[WHOLE, WHOLE] + [ANY] * 3,
        out_specs=ANY,
        out_shape=jax.ShapeDtypeStruct((2, slab, lanes * CHUNKS), jnp.float32),
        scratch_shapes=[pltpu.VMEM(s, jnp.float32) for s in shapes]
        + [
            dma((3, CHUNKS)),
            dma((pencils, CHUNKS)),
            dma((pencils, CHUNKS)),
            dma((2, pencils - 1, CHUNKS)),
            dma((2, pencils - 1, CHUNKS)),
            dma((CHUNKS,)),
        ],
        compiler_params=pltpu.CompilerParams(
            collective_id=1, has_side_effects=True, vmem_limit_bytes=VMEM
        ),
    )(*table, potential, own, far)


def schedule(kpts, bands, sets):
    count = kpts * bands
    if count != 8 or bands != 2 or sets < 4:
        raise NotImplementedError
    x, core, y = 4, 2, 1
    rows = [
        (x, y | core, x | core, False),
        (x | core, y, core | y, False),
        (x | y, core, core | x, False),
        (x | y | core, core, core, True),
    ]
    partner = np.zeros((4, count), np.int32)
    packed = np.zeros((4, count), np.int32)
    for p, (even, odd, mask, diagonal) in enumerate(rows):
        for g in range(count):
            side = bin(g & mask).count("1") % 2
            partner[p, g] = g ^ (odd if side else even)
            packed[p, g] = int(diagonal and side == 1)
    return partner, packed


def body(orbitals, kcoords):
    kpts = kcoords.shape[0]
    bands = lax.axis_size("band") * orbitals.shape[2]
    pencils = lax.axis_size("pencil")
    slab, plane = orbitals.shape[3:]
    grid = slab * pencils
    count = kpts * bands
    partner, packed = schedule(kpts, bands, pencils)
    axes = ("kpair", "band", "pencil")
    pencil = lax.axis_index("pencil")
    orbital = lax.axis_index("kpair") * bands + lax.axis_index("band")
    row = pencil % 4
    far = jnp.asarray(partner)[row, orbital]
    flag = jnp.where(pencil < 4, jnp.asarray(packed)[row, orbital], 0).reshape(1)
    active = (pencil < 4).astype(jnp.float32)
    coords = kcoords.astype(jnp.float32) * 0.25
    shift = coords[orbital // bands] - coords[far // bands]
    shift = jnp.where(flag[0] > 0, 0.0, shift)
    fetch = [
        (int(partner[p % 4, g]) * pencils + p, g * pencils + p)
        for p in range(pencils)
        for g in range(count)
    ]
    give = [(b, a) for a, b in fetch]
    all_tables = tables(grid)
    padded = -(-grid // LANES) * LANES
    lanes = plane // CHUNKS
    part = lanes // grid

    scale = -1.0 / (count * grid**3)

    step = math.lcm(grid, LANES)
    if pencils == 4 and slab % 8 == 0 and lanes % step == 0 and part % 8 == 0:
        own, other, spectrum = gathered(orbitals[:, 0, 0], all_tables[0], pencils)
        potential = filtered([spectrum[None]], kcoords, all_tables, grid, scale)[0]
        result = scattered(potential[0], own, other, all_tables[1], pencils)
        return result[:, None, None]

    own_chunks, far_chunks, spectra = [], [], []
    for j in range(CHUNKS):
        piece = orbitals[:, 0, 0, :, j * lanes : (j + 1) * lanes]
        own = lax.all_gather(piece, "pencil", axis=1, tiled=True)
        other = lax.ppermute(own, axes, fetch)
        own_chunks.append(own)
        far_chunks.append(other)
        (spectrum,) = along_x(density_kernel, 1, flag, all_tables[0], own, other)
        spectrum = spectrum.reshape(2, grid, part, grid)
        spectra.append(jnp.pad(spectrum, ((0, 0), (0, 0), (0, 0), (0, padded - grid))))

    potentials = filtered([jnp.stack(spectra)], shift, all_tables, grid, scale)[0]
    results = []
    for j in range(CHUNKS):
        potential = potentials[j][..., :grid].reshape(2, grid, lanes)
        direct, reverse = along_x(
            apply_kernel, 2, flag, all_tables[1], potential, own_chunks[j], far_chunks[j]
        )
        total = direct + lax.ppermute(reverse, axes, give)
        if pencils > 4:
            total = total * active
        results.append(lax.psum_scatter(total, "pencil", scatter_dimension=1, tiled=True))
    return jnp.concatenate(results, axis=2)[:, None, None]


def solution(mesh):
    in_specs = (P(None, "kpair", "band", "pencil", None), P())
    out_specs = P(None, "kpair", "band", "pencil", None)
    return jax.shard_map(body, mesh=mesh, in_specs=in_specs, out_specs=out_specs, check_vma=False)
```
